32 devices in a mesh: seq: 16 (over z, y, x), head: 2 (over core).
Axes of the slice: x: 2, y: 2, z: 4, core: 2. Of those that a mesh axis runs over, the one named last changes fastest.
Arguments:
- queries: bfloat16 [16384, 1024], P('seq', 'head'), may hold values from -14 to 14
- key_rows: bfloat16 [16384, 1024], P('seq', 'head'), may hold values from -14 to 14
- value_rows: bfloat16 [16384, 1024], P('seq', 'head'), may hold values from -8 to 8
- out_weight: bfloat16 [1024, 1024], P('head'), may hold values from -0.1875 to 0.1875
Outputs:
- mixed: bfloat16 [16384, 1024], P('seq', 'head')
The draws below stay inside these ranges and needn't reach their ends.
All inputs are finite; a program needn't handle non-finite values.
Results may differ from the reference program's by a relative error of at most 0.012.
Values may be sent and summed in bfloat16 or wider, within the bound.
A program may use at most 128 MiB of HBM per device.

```python
import jax
import jax.numpy as jnp
from jax import lax

D = 1024
HEADS = 16
HEAD_DIM = 64
BLOCK = 256
LEVELS = 6
TOKENS = 16384
N_HEAD = 2


def base_field(key, offset_scale):
    noise_key, offset_key = jax.random.split(key, 2)
    columns = HEADS * HEAD_DIM
    noise_part = jnp.clip(jax.random.normal(noise_key, (TOKENS, columns), jnp.float32), -4.0, 4.0)
    offsets = jnp.clip(jax.random.normal(offset_key, (TOKENS // (2 * BLOCK), columns), jnp.float32), -2.0, 2.0)
    return noise_part + jnp.repeat(offsets * offset_scale, 2 * BLOCK, axis=0)


def draw_queries(key, part):
    field_rows = base_field(jax.random.fold_in(key, 1), 0.5)
    return field_rows.astype(jnp.bfloat16)


def draw_key_rows(key, part):
    field_rows = base_field(jax.random.fold_in(key, 2), 0.5)
    return field_rows.astype(jnp.bfloat16)


def draw_value_rows(key, part):
    field_rows = base_field(jax.random.fold_in(key, 3), 1.0)
    return field_rows.astype(jnp.bfloat16)


def levels(rng, dims, cuts, least, high):
    loudness, own = 1.0, jax.random.fold_in(rng, 6)
    for axis_at, parts in cuts:
        steps = jnp.exp(jax.random.uniform(jax.random.fold_in(own, axis_at), (parts,), jnp.float32, least / len(cuts), high / len(cuts)))
        loudness = loudness * jnp.repeat(steps, dims[axis_at] // parts).reshape([-1 if axis == axis_at else 1 for axis in range(len(dims))])
    return loudness


def normal_values(key, extent, width, reach, shards=(), held_as=jnp.bfloat16):
    gain = levels(key, extent, shards, -0.22, 0.18) if shards else 1.0
    entries = jax.random.normal(key, extent, jnp.float32) * width * gain
    return jnp.minimum(jnp.maximum(entries, -reach), reach).astype(held_as)


def setup_inputs(seed: int = 0) -> dict:
    arg_keys = jax.random.split(jax.random.key(seed), 5)
    return {
        "queries": draw_queries(jax.random.fold_in(arg_keys[4], 71), 0),
        "key_rows": draw_key_rows(jax.random.fold_in(arg_keys[4], 71), 0),
        "value_rows": draw_value_rows(jax.random.fold_in(arg_keys[4], 71), 0),
        "out_weight": normal_values(arg_keys[3], (HEADS * HEAD_DIM, D), (HEADS * HEAD_DIM) ** -0.5, 0.1875, ((0, 2),)),
    }


LOG_TWO = 0.6931471805599453
NEG_LARGE = -1.0e30


def coarsen(rows_in):
    row_count = rows_in.shape[-2]
    widened = rows_in.astype(jnp.float32).reshape(rows_in.shape[:-2] + (row_count // 2, 2, rows_in.shape[-1]))
    return ((widened[..., 0, :] + widened[..., 1, :]) * 0.5).astype(jnp.bfloat16)


def level_attention(query_level, key_level, value_level, height):
    length = query_level.shape[0]
    blocks = length // BLOCK
    padding = jnp.zeros((BLOCK, HEADS * HEAD_DIM), jnp.bfloat16)
    key_blocks = jnp.concatenate([padding, key_level, padding], 0).reshape(blocks + 2, BLOCK, HEADS, HEAD_DIM)
    value_blocks = jnp.concatenate([padding, value_level, padding], 0).reshape(blocks + 2, BLOCK, HEADS, HEAD_DIM)
    query_blocks = query_level.reshape(blocks, BLOCK, HEADS, HEAD_DIM)
    offsets = [0, 1, 2] if height == 0 else [0, 2]

    def one_block(block_index):
        query_here = query_blocks[block_index].astype(jnp.float32)
        keys_here = jnp.concatenate([key_blocks[block_index + offset] for offset in offsets], 0).astype(jnp.float32)
        values_here = jnp.concatenate([value_blocks[block_index + offset] for offset in offsets], 0).astype(jnp.float32)
        block_flags = jnp.stack([(block_index + offset - 1 >= 0) & (block_index + offset - 1 < blocks) for offset in offsets])
        valid_keys = jnp.repeat(block_flags, BLOCK)
        scores = jnp.einsum("qhd,khd->hqk", query_here, keys_here) * HEAD_DIM ** -0.5 + height * LOG_TWO
        scores = jnp.where(valid_keys[None, None, :], scores, NEG_LARGE)
        row_peak = jnp.max(scores, axis=-1)
        weights = jnp.exp(scores - row_peak[..., None])
        row_total = jnp.sum(weights, axis=-1)
        rounded = lax.optimization_barrier(weights.astype(jnp.bfloat16)).astype(jnp.float32)
        numerator = jnp.einsum("hqk,khd->qhd", rounded, values_here)
        return row_peak.T, row_total.T, numerator

    row_peak, row_total, numerator = lax.map(one_block, jnp.arange(blocks, dtype=jnp.int32))
    return (row_peak.reshape(length, HEADS), row_total.reshape(length, HEADS),
            numerator.reshape(length, HEADS, HEAD_DIM))


def reference(queries, key_rows, value_rows, out_weight):
    tokens_all = queries.shape[0]
    query_level, key_level, value_level = queries, key_rows, value_rows
    run_peak = None
    run_total = None
    run_numer = None
    for height in range(LEVELS):
        if height > 0:
            query_level = coarsen(query_level)
            key_level = coarsen(key_level)
            value_level = coarsen(value_level)
        row_peak, row_total, numerator = level_attention(query_level, key_level, value_level, height)
        factor = 2 ** height
        row_peak = jnp.repeat(row_peak, factor, axis=0)
        row_total = jnp.repeat(row_total, factor, axis=0)
        numerator = jnp.repeat(numerator, factor, axis=0)
        if height == 0:
            run_peak, run_total, run_numer = row_peak, row_total, numerator
        else:
            newest = jnp.maximum(run_peak, row_peak)
            keep_scale = jnp.exp(run_peak - newest)
            fresh_scale = jnp.exp(row_peak - newest)
            run_total = run_total * keep_scale + row_total * fresh_scale
            run_numer = run_numer * keep_scale[..., None] + numerator * fresh_scale[..., None]
            run_peak = newest
    attended = (run_numer / run_total[..., None]).astype(jnp.bfloat16).reshape(tokens_all, HEADS * HEAD_DIM)
    group_width = HEADS * HEAD_DIM // N_HEAD
    summed = jnp.zeros((tokens_all, D), jnp.float32)
    for head_group in range(N_HEAD):
        partial_term = jnp.dot(attended[:, head_group * group_width:(head_group + 1) * group_width],
                               out_weight[head_group * group_width:(head_group + 1) * group_width],
                               preferred_element_type=jnp.float32)
        summed = summed + lax.optimization_barrier(partial_term.astype(jnp.bfloat16)).astype(jnp.float32)
    return summed.astype(jnp.bfloat16)
```

```python
import functools
import math

import jax
import jax.numpy as jnp
from jax import lax
from jax.experimental import pallas as pl
from jax.experimental.pallas import tpu as pltpu
from jax.sharding import PartitionSpec as P

HEAD_DIM = 64
BLOCK = 256
LEVELS = 6
LOG_TWO = 0.6931471805599453
NEG_LARGE = -1e30
LANES = 128
MESH = pl.DeviceIdType.MESH
BF16 = jnp.bfloat16
F32 = jnp.float32


def pool(x):
    rows = x.shape[0]
    r = lax.broadcasted_iota(jnp.int32, (rows // 2, rows), 0)
    c = lax.broadcasted_iota(jnp.int32, (rows // 2, rows), 1)
    mat = jnp.where((c == 2 * r) | (c == 2 * r + 1), 0.5, 0.0).astype(BF16)
    return jnp.dot(mat, x, preferred_element_type=F32).astype(BF16)


def kernel(n_seq, tok, pairs, q_hbm, k_hbm, v_hbm, w_hbm, o_ref, *scratch):
    scratch = list(scratch)

    def take(count):
        out = scratch[:count]
        del scratch[:count]
        return out

    kv = take(LEVELS)
    qs = take(LEVELS)
    nums = take(LEVELS)
    tots = take(LEVELS)
    mxs = take(LEVELS)
    tmp, att, w_s, psend, precv, load_sem, send_sem, recv_sem, psend_sem, precv_sem = scratch

    me = lax.axis_index("seq")
    head = lax.axis_index("head")
    rows_of = [tok >> l for l in range(LEVELS)]
    span_of = [max(1, BLOCK // r) for r in rows_of]
    half = o_ref.shape[1]

    loads = []
    for p in range(pairs):
        cols = pl.ds(p * LANES, LANES)
        loads.append(pltpu.make_async_copy(
            k_hbm.at[:, cols], kv[0].at[0, p, pl.ds(BLOCK, tok)], load_sem.at[0, p]))
        loads.append(pltpu.make_async_copy(
            v_hbm.at[:, cols], kv[0].at[1, p, pl.ds(BLOCK, tok)], load_sem.at[1, p]))
        loads.append(pltpu.make_async_copy(q_hbm.at[:, cols], qs[0].at[p], load_sem.at[2, p]))
    w_load = pltpu.make_async_copy(w_hbm, w_s, load_sem.at[3, 0])
    for c in loads:
        c.start()
    w_load.start()

    top = span_of[-1]
    top_block = me // top
    top_blocks = n_seq // top
    barrier = pltpu.get_barrier_semaphore()
    pl.semaphore_signal(barrier, inc=1, device_id={"head": 1 - head}, device_id_type=MESH)
    for delta in (-1, 0, 1):
        there = top_block + delta

        @pl.when((there >= 0) & (there < top_blocks))
        def _():
            for j in range(top):
                other = there * top + j

                @pl.when(other != me)
                def _():
                    pl.semaphore_signal(
                        barrier, inc=1, device_id={"seq": other}, device_id_type=MESH)

    exists = []
    for l in range(LEVELS):
        block = me // span_of[l]
        has_left = block >= 1
        has_right = block + 1 < n_seq // span_of[l]
        exists.append((has_left, has_right))
        r = rows_of[l]

        @pl.when(jnp.logical_not(has_left))
        def _():
            kv[l][:, :, pl.ds(0, BLOCK), :] = jnp.zeros((2, pairs, BLOCK, LANES), BF16)

        @pl.when(jnp.logical_not(has_right))
        def _():
            kv[l][:, :, pl.ds(BLOCK + r, BLOCK), :] = jnp.zeros((2, pairs, BLOCK, LANES), BF16)

    around = jnp.minimum(top_block, 1) + jnp.minimum(top_blocks - 1 - top_block, 1)
    pl.semaphore_wait(barrier, top + top * around)

    def copies(l, side):
        r, n = rows_of[l], span_of[l]
        block, place = me // n, lax.rem(me, n)
        if r >= BLOCK:
            length = BLOCK if l == 0 else BLOCK // 2
            if side == 1:
                src, dst = BLOCK + r - BLOCK, 0
            else:
                src = BLOCK + BLOCK - length
                dst = BLOCK + r + BLOCK - length
        else:
            length = r
            src = BLOCK
            dst = place * r + (0 if side == 1 else BLOCK + r)
            dst = pl.multiple_of(dst, r)
        out = []
        for j in range(n):
            target = (block + (1 if side == 1 else -1)) * n + j
            out.append(pltpu.make_async_remote_copy(
                src_ref=kv[l].at[:, :, pl.ds(src, length)],
                dst_ref=kv[l].at[:, :, pl.ds(dst, length)],
                send_sem=send_sem.at[l, side, j],
                recv_sem=recv_sem.at[l, 1 - side],
                device_id={"seq": target},
                device_id_type=MESH))
        return out

    def start(l):
        for side in (0, 1):
            @pl.when(exists[l][side])
            def _():
                for c in copies(l, side):
                    c.start()

    def wait(l):
        r = rows_of[l]
        for side in (0, 1):
            length = BLOCK // 2 if (r >= BLOCK and l > 0) else BLOCK
            if side == 0:
                at = 0
            else:
                at = BLOCK + r + BLOCK - length

            @pl.when(exists[l][side])
            def _():
                region = kv[l].at[:, :, pl.ds(at, length)]
                pltpu.make_async_copy(region, region, recv_sem.at[l, side]).wait()

    for c in loads:
        c.wait()
    start(0)

    for l in range(1, LEVELS):
        r = rows_of[l]
        step = min(BLOCK, 2 * r)

        def coarse(p, _, l=l, r=r, step=step):
            for at in range(0, 2 * r, step):
                for s in range(2):
                    kv[l][s, p, pl.ds(BLOCK + at // 2, step // 2), :] = pool(
                        kv[l - 1][s, p, pl.ds(BLOCK + at, step), :])
                qs[l][p, pl.ds(at // 2, step // 2), :] = pool(qs[l - 1][p, pl.ds(at, step), :])
            return 0

        lax.fori_loop(0, pairs, coarse, 0)
        start(l)

    lane = lax.broadcasted_iota(jnp.int32, (1, LANES), 1)
    low = lane < HEAD_DIM
    masks = [jnp.where(low, 1.0, 0.0).astype(BF16), jnp.where(low, 0.0, 1.0).astype(BF16)]
    scale = HEAD_DIM ** -0.5

    def bias_of(valid):
        return jnp.where(valid, 0.0, NEG_LARGE).astype(F32)

    def attend(l, j, p):
        r = rows_of[l]
        size = min(BLOCK, r)
        has_left, has_right = exists[l]
        blocks = max(1, r // BLOCK)
        if r >= BLOCK:
            left_at, right_at = j * BLOCK, (j + 2) * BLOCK
        else:
            left_at, right_at = 0, BLOCK + r
        left_bias = bias_of(has_left) if j == 0 else None
        right_bias = bias_of(has_right) if j == blocks - 1 else None
        if l == 0:
            segments = [(left_at, left_bias), (left_at + BLOCK, None), (right_at, right_bias)]
        else:
            segments = [(left_at, left_bias), (right_at, right_bias)]
        q = qs[l][p, pl.ds(j * BLOCK, size), :]
        ks = [kv[l][0, p, pl.ds(at, BLOCK), :] for at, _ in segments]
        vs = [kv[l][1, p, pl.ds(at, BLOCK), :] for at, _ in segments]
        accs, peaks = [], []
        for e in (0, 1):
            mine = masks[e]
            other = masks[1 - e]
            q_e = q * (mine * scale) + other
            k_e = []
            for (at, bias), k in zip(segments, ks):
                k = k * mine
                if bias is not None:
                    k = k + (other.astype(F32) * bias).astype(BF16)
                k_e.append(k)
            k_e = jnp.concatenate(k_e, axis=0)
            v_e = jnp.concatenate([v * mine + other for v in vs], axis=0)
            s = lax.dot_general(q_e, k_e, (((1,), (1,)), ((), ())), preferred_element_type=F32)
            peak = jnp.max(s, axis=1, keepdims=True)
            weights = jnp.exp(s - peak).astype(BF16)
            accs.append(jnp.dot(weights, v_e, preferred_element_type=F32))
            peaks.append(peak)
        at = pl.ds(j * BLOCK, size)
        nums[l][p, at, :] = jnp.where(low, accs[0], accs[1])
        tots[l][p, at, :] = pltpu.roll(jnp.where(low, accs[1], accs[0]), HEAD_DIM, 1)
        mxs[l][p, at, :] = jnp.where(low, peaks[0], peaks[1]) + l * LOG_TWO

    def phase(l, which):
        def body(p, _):
            for j in which:
                attend(l, j, p)
            return 0

        lax.fori_loop(0, pairs, body, 0)

    def near(l):
        r, below = rows_of[l], rows_of[l - 1]

        def body(p, _):
            for s in range(2):
                kv[l][s, p, pl.ds(BLOCK // 2, BLOCK // 2), :] = pool(
                    kv[l - 1][s, p, pl.ds(0, BLOCK), :])
                kv[l][s, p, pl.ds(BLOCK + r, BLOCK // 2), :] = pool(
                    kv[l - 1][s, p, pl.ds(BLOCK + below, BLOCK), :])
            return 0

        lax.fori_loop(0, pairs, body, 0)

    blocks0 = max(1, tok // BLOCK)
    inner = list(range(1, blocks0 - 1))
    outer = [j for j in range(blocks0) if j not in inner]
    for j in inner:
        phase(0, [j])
    wait(0)
    for j in outer:
        phase(0, [j])
    for l in range(1, LEVELS):
        wait(l)
        if rows_of[l] >= BLOCK:
            near(l)
        for j in range(max(1, rows_of[l] // BLOCK)):
            phase(l, [j])

    def join(p, _):
        cur = (nums[-1][p], tots[-1][p], mxs[-1][p])
        for l in range(LEVELS - 2, -1, -1):
            r = rows_of[l]
            for i, x in enumerate(cur):
                tmp[i, pl.ds(0, r // 2, stride=2), :] = x
                tmp[i, pl.ds(1, r // 2, stride=2), :] = x
            num, tot, peak = (tmp[i, pl.ds(0, r), :] for i in range(3))
            peak_l = mxs[l][p]
            newest = jnp.maximum(peak, peak_l)
            keep = jnp.exp(peak - newest)
            fresh = jnp.exp(peak_l - newest)
            cur = (num * keep + nums[l][p] * fresh, tot * keep + tots[l][p] * fresh, newest)
        att[:, pl.ds(pl.multiple_of(p * LANES, LANES), LANES)] = (cur[0] / cur[1]).astype(BF16)
        return 0

    lax.fori_loop(0, pairs, join, 0)

    w_load.wait()
    chunk = min(BLOCK, tok)
    chunks = tok // chunk
    other_cols = pl.ds(pl.multiple_of((1 - head) * half, half), half)
    own_cols = pl.ds(pl.multiple_of(head * half, half), half)

    def part_copy(c):
        at = pl.ds(c * chunk, chunk)
        return pltpu.make_async_remote_copy(
            src_ref=psend.at[at], dst_ref=precv.at[at],
            send_sem=psend_sem.at[c], recv_sem=precv_sem.at[c],
            device_id={"head": 1 - head}, device_id_type=MESH)

    for c in range(chunks):
        at = pl.ds(c * chunk, chunk)
        psend[at, :] = jnp.dot(
            att[at, :], w_s[:, other_cols], preferred_element_type=F32).astype(BF16)
        part_copy(c).start()
    for c in range(chunks):
        at = pl.ds(c * chunk, chunk)
        own = jnp.dot(att[at, :], w_s[:, own_cols], preferred_element_type=F32).astype(BF16)
        part_copy(c).wait_recv()
        o_ref[at, :] = (own.astype(F32) + precv[at, :].astype(F32)).astype(BF16)
    for c in range(chunks):
        part_copy(c).wait_send()
    for l in range(LEVELS):
        for side in (0, 1):
            @pl.when(exists[l][side])
            def _():
                for c in copies(l, side):
                    c.wait_send()


def local(n_seq, queries, key_rows, value_rows, out_weight):
    tok, columns = queries.shape
    pairs = columns // LANES
    width = out_weight.shape[1]
    half = width // 2
    rows_of = [tok >> l for l in range(LEVELS)]
    top = max(1, BLOCK // rows_of[-1])
    chunks = tok // min(BLOCK, tok)
    results = [pltpu.VMEM((pairs, r, LANES), F32) for r in rows_of]
    scratch = (
        [pltpu.VMEM((2, pairs, r + 2 * BLOCK, LANES), BF16) for r in rows_of]
        + [pltpu.VMEM((pairs, r, LANES), BF16) for r in rows_of]
        + results * 3
        + [
            pltpu.VMEM((3, tok, LANES), F32),
            pltpu.VMEM((tok, columns), BF16),
            pltpu.VMEM(out_weight.shape, BF16),
            pltpu.VMEM((tok, half), BF16),
            pltpu.VMEM((tok, half), BF16),
            pltpu.SemaphoreType.DMA((4, pairs)),
            pltpu.SemaphoreType.DMA((LEVELS, 2, top)),
            pltpu.SemaphoreType.DMA((LEVELS, 2)),
            pltpu.SemaphoreType.DMA((chunks,)),
            pltpu.SemaphoreType.DMA((chunks,)),
        ]
    )
    return pl.pallas_call(
        functools.partial(kernel, n_seq, tok, pairs),
        out_shape=jax.ShapeDtypeStruct((tok, half), BF16),
        in_specs=[pl.BlockSpec(memory_space=pl.ANY)] * 4,
        out_specs=pl.BlockSpec(memory_space=pltpu.VMEM),
        scratch_shapes=scratch,
        compiler_params=pltpu.CompilerParams(
            collective_id=0, has_side_effects=True, vmem_limit_bytes=56 * 1024 * 1024),
    )(queries, key_rows, value_rows, out_weight)


def solution(mesh):
    return jax.shard_map(
        functools.partial(local, mesh.shape["seq"]),
        mesh=mesh,
        in_specs=(P("seq", "head"), P("seq", "head"), P("seq", "head"), P("head", None)),
        out_specs=P("seq", "head"),
        check_vma=False,
    )
```

```python
import functools
import math

import jax
import jax.numpy as jnp
from jax import lax
from jax.experimental import pallas as pl
from jax.experimental.pallas import tpu as pltpu
from jax.sharding import PartitionSpec as P

HEAD_DIM = 64
BLOCK = 256
LEVELS = 6
LOG_TWO = 0.6931471805599453
NEG_LARGE = -1e30
LANES = 128
MESH = pl.DeviceIdType.MESH
BF16 = jnp.bfloat16
F32 = jnp.float32


def pool(x):
    rows = x.shape[0]
    r = lax.broadcasted_iota(jnp.int32, (rows // 2, rows), 0)
    c = lax.broadcasted_iota(jnp.int32, (rows // 2, rows), 1)
    mat = jnp.where((c == 2 * r) | (c == 2 * r + 1), 0.5, 0.0).astype(BF16)
    return jnp.dot(mat, x, preferred_element_type=F32).astype(BF16)


def kernel(n_seq, tok, pairs, q_hbm, k_hbm, v_hbm, w_hbm, o_ref, *scratch):
    scratch = list(scratch)

    def take(count):
        out = scratch[:count]
        del scratch[:count]
        return out

    kv = take(LEVELS)
    qs = take(LEVELS)
    nums = take(LEVELS)
    tots = take(LEVELS)
    mxs = take(LEVELS)
    tmp, att, w_s, psend, precv, load_sem, send_sem, recv_sem, pair_sem, psend_sem, precv_sem = scratch

    me = lax.axis_index("seq")
    head = lax.axis_index("head")
    rows_of = [tok >> l for l in range(LEVELS)]
    span_of = [max(1, BLOCK // r) for r in rows_of]
    half = o_ref.shape[1]
    first_up = next(l for l in range(LEVELS) if span_of[l] > 1)

    loads = []
    for p in range(pairs):
        cols = pl.ds(p * LANES, LANES)
        loads.append(pltpu.make_async_copy(
            k_hbm.at[:, cols], kv[0].at[0, p, pl.ds(BLOCK, tok)], load_sem.at[0, p]))
        loads.append(pltpu.make_async_copy(
            v_hbm.at[:, cols], kv[0].at[1, p, pl.ds(BLOCK, tok)], load_sem.at[1, p]))
        loads.append(pltpu.make_async_copy(q_hbm.at[:, cols], qs[0].at[p], load_sem.at[2, p]))
    w_load = pltpu.make_async_copy(w_hbm, w_s, load_sem.at[3, 0])
    for c in loads:
        c.start()
    w_load.start()

    exists = []
    for l in range(LEVELS):
        n = span_of[l]
        exists.append((me >= n, me + n < n_seq))

    barrier = pltpu.get_barrier_semaphore()
    pl.semaphore_signal(barrier, inc=1, device_id={"head": 1 - head}, device_id_type=MESH)
    greeted = 1
    for n in sorted(set(span_of)):
        for there in (me - n, me + n):
            inside = (there >= 0) & (there < n_seq)
            greeted = greeted + jnp.where(inside, 1, 0)

            @pl.when(inside)
            def _():
                pl.semaphore_signal(
                    barrier, inc=1, device_id={"seq": there}, device_id_type=MESH)

    for l in range(LEVELS):
        has_left, has_right = exists[l]
        r = max(rows_of[l], BLOCK)

        @pl.when(jnp.logical_not(has_left))
        def _():
            kv[l][:, :, pl.ds(0, BLOCK), :] = jnp.zeros((2, pairs, BLOCK, LANES), BF16)

        @pl.when(jnp.logical_not(has_right))
        def _():
            kv[l][:, :, pl.ds(BLOCK + r, BLOCK), :] = jnp.zeros((2, pairs, BLOCK, LANES), BF16)

    pl.semaphore_wait(barrier, greeted)

    HALF = BLOCK // 2

    def child(l):
        return lax.rem(me // span_of[l - 1], 2)

    def plans(l, side):
        r = max(rows_of[l], BLOCK)
        far = BLOCK + r
        if l == 0 or l == first_up:
            return [(None, BLOCK, r, 0) if side else (None, BLOCK, BLOCK, far)]
        part = (None, HALF, r, 0) if side else (None, HALF, BLOCK + HALF, far + HALF)
        if l < first_up:
            return [part]
        whole = (None, BLOCK, r, 0) if side else (None, BLOCK, BLOCK, far)
        c = child(l)
        whole_if, part_if = (c == 1, c == 0) if side else (c == 0, c == 1)
        return [(whole_if,) + whole[1:], (part_if,) + part[1:]]

    def each(l, side, act):
        for cond, length, src, dst in plans(l, side):
            n = span_of[l]
            on = exists[l][side] if cond is None else exists[l][side] & cond

            @pl.when(on)
            def _():
                act(pltpu.make_async_remote_copy(
                    src_ref=kv[l].at[:, :, pl.ds(src, length)],
                    dst_ref=kv[l].at[:, :, pl.ds(dst, length)],
                    send_sem=send_sem.at[l, side],
                    recv_sem=recv_sem.at[l, 1 - side],
                    device_id={"seq": me + n if side else me - n},
                    device_id_type=MESH))

    def start(l):
        for side in (0, 1):
            each(l, side, lambda copy: copy.start())

    def wait(l):
        for side in (0, 1):
            for cond, length, _, dst in plans(l, 1 - side):
                on = exists[l][side] if cond is None else exists[l][side] & cond

                @pl.when(on)
                def _():
                    region = kv[l].at[:, :, pl.ds(dst, length)]
                    pltpu.make_async_copy(region, region, recv_sem.at[l, side]).wait()

    place = lax.rem(me, 2)
    part_at = pl.ds(pl.multiple_of(BLOCK + place * HALF, HALF), HALF)
    pair_copy = pltpu.make_async_remote_copy(
        src_ref=kv[first_up].at[:, :, part_at],
        dst_ref=kv[first_up].at[:, :, part_at],
        send_sem=pair_sem.at[0], recv_sem=pair_sem.at[1],
        device_id={"seq": me + 1 - 2 * place}, device_id_type=MESH)
    other_at = pl.ds(pl.multiple_of(BLOCK + (1 - place) * HALF, HALF), HALF)

    def pair_wait():
        region = kv[first_up].at[:, :, other_at]
        pltpu.make_async_copy(region, region, pair_sem.at[1]).wait()

    for c in loads:
        c.wait()
    start(0)

    def coarse_keys(p, _):
        for l in range(1, first_up):
            for at in range(0, 2 * rows_of[l], BLOCK):
                for s in range(2):
                    kv[l][s, p, pl.ds(BLOCK + at // 2, HALF), :] = pool(
                        kv[l - 1][s, p, pl.ds(BLOCK + at, BLOCK), :])
        for s in range(2):
            kv[first_up][s, p, part_at, :] = pool(kv[first_up - 1][s, p, pl.ds(BLOCK, BLOCK), :])
        return 0

    lax.fori_loop(0, pairs, coarse_keys, 0)
    pair_copy.start()
    for l in range(1, first_up):
        start(l)

    def coarse_queries(p, _):
        for l in range(1, LEVELS):
            r = rows_of[l]
            step = min(BLOCK, 2 * r)
            for at in range(0, 2 * r, step):
                qs[l][p, pl.ds(at // 2, step // 2), :] = pool(qs[l - 1][p, pl.ds(at, step), :])
        return 0

    lax.fori_loop(0, pairs, coarse_queries, 0)

    lane = lax.broadcasted_iota(jnp.int32, (1, LANES), 1)
    low = lane < HEAD_DIM
    masks = [jnp.where(low, 1.0, 0.0).astype(BF16), jnp.where(low, 0.0, 1.0).astype(BF16)]
    scale = HEAD_DIM ** -0.5

    def bias_of(valid):
        return jnp.where(valid, 0.0, NEG_LARGE).astype(F32)

    def attend(l, j, p):
        r = rows_of[l]
        size = min(BLOCK, r)
        has_left, has_right = exists[l]
        blocks = max(1, r // BLOCK)
        if r >= BLOCK:
            left_at, right_at = j * BLOCK, (j + 2) * BLOCK
        else:
            left_at, right_at = 0, 2 * BLOCK
        left_bias = bias_of(has_left) if j == 0 else None
        right_bias = bias_of(has_right) if j == blocks - 1 else None
        if l == 0:
            segments = [(left_at, left_bias), (left_at + BLOCK, None), (right_at, right_bias)]
        else:
            segments = [(left_at, left_bias), (right_at, right_bias)]
        q = qs[l][p, pl.ds(j * BLOCK, size), :]
        ks = [kv[l][0, p, pl.ds(at, BLOCK), :] for at, _ in segments]
        vs = [kv[l][1, p, pl.ds(at, BLOCK), :] for at, _ in segments]
        accs, peaks = [], []
        for e in (0, 1):
            mine = masks[e]
            other = masks[1 - e]
            q_e = q * (mine * scale) + other
            k_e = []
            for (at, bias), k in zip(segments, ks):
                k = k * mine
                if bias is not None:
                    k = k + (other.astype(F32) * bias).astype(BF16)
                k_e.append(k)
            k_e = jnp.concatenate(k_e, axis=0)
            v_e = jnp.concatenate([v * mine + other for v in vs], axis=0)
            s = lax.dot_general(q_e, k_e, (((1,), (1,)), ((), ())), preferred_element_type=F32)
            peak = jnp.max(s, axis=1, keepdims=True)
            weights = jnp.exp(s - peak).astype(BF16)
            accs.append(jnp.dot(weights, v_e, preferred_element_type=F32))
            peaks.append(peak)
        at = pl.ds(j * BLOCK, size)
        nums[l][p, at, :] = jnp.where(low, accs[0], accs[1])
        tots[l][p, at, :] = pltpu.roll(jnp.where(low, accs[1], accs[0]), HEAD_DIM, 1)
        mxs[l][p, at, :] = jnp.where(low, peaks[0], peaks[1]) + l * LOG_TWO

    def phase(l, which):
        def body(p, _):
            for j in which:
                attend(l, j, p)
            return 0

        lax.fori_loop(0, pairs, body, 0)

    def near(l):
        r, below = rows_of[l], rows_of[l - 1]

        def body(p, _):
            for s in range(2):
                kv[l][s, p, pl.ds(BLOCK // 2, BLOCK // 2), :] = pool(
                    kv[l - 1][s, p, pl.ds(0, BLOCK), :])
                kv[l][s, p, pl.ds(BLOCK + r, BLOCK // 2), :] = pool(
                    kv[l - 1][s, p, pl.ds(BLOCK + below, BLOCK), :])
            return 0

        lax.fori_loop(0, pairs, body, 0)

    def gather(l):
        c = child(l)
        own = pl.ds(pl.multiple_of(BLOCK + c * HALF, HALF), HALF)
        sibling = pl.ds(pl.multiple_of(BLOCK + (1 - c) * HALF, HALF), HALF)
        sibling_from = pl.ds(pl.multiple_of((1 - c) * 2 * BLOCK, BLOCK), BLOCK)
        beside = pl.ds(pl.multiple_of(HALF + c * 3 * HALF, HALF), HALF)
        beside_from = pl.ds(pl.multiple_of(c * 2 * BLOCK, BLOCK), BLOCK)

        def body(p, _):
            for s in range(2):
                below = kv[l - 1]
                kv[l][s, p, own, :] = pool(below[s, p, pl.ds(BLOCK, BLOCK), :])
                kv[l][s, p, sibling, :] = pool(below[s, p, sibling_from, :])
                kv[l][s, p, beside, :] = pool(below[s, p, beside_from, :])
            return 0

        lax.fori_loop(0, pairs, body, 0)

    blocks0 = tok // BLOCK
    inner = list(range(1, blocks0 - 1))
    outer = [j for j in range(blocks0) if j not in inner]
    pieces = inner[:1], inner[1:], outer[:1], outer[1:]
    for j in pieces[0]:
        phase(0, [j])
    pair_wait()
    start(first_up)
    for j in pieces[1]:
        phase(0, [j])
    wait(0)
    for j in pieces[2]:
        phase(0, [j])
    ups = list(range(first_up, LEVELS))
    wait(first_up)
    if len(ups) > 1:
        gather(ups[1])
        start(ups[1])
    for j in pieces[3]:
        phase(0, [j])
    for l in range(1, first_up):
        wait(l)
        near(l)
        for j in range(rows_of[l] // BLOCK):
            phase(l, [j])
        if l + 1 < len(ups):
            wait(ups[l])
            gather(ups[l + 1])
            start(ups[l + 1])
    for l in ups[:-1]:
        phase(l, [0])
    wait(ups[-1])
    phase(ups[-1], [0])

    def join(p, _):
        cur = (nums[-1][p], tots[-1][p], mxs[-1][p])
        for l in range(LEVELS - 2, -1, -1):
            r = rows_of[l]
            for i, x in enumerate(cur):
                tmp[i, pl.ds(0, r // 2, stride=2), :] = x
                tmp[i, pl.ds(1, r // 2, stride=2), :] = x
            num, tot, peak = (tmp[i, pl.ds(0, r), :] for i in range(3))
            peak_l = mxs[l][p]
            newest = jnp.maximum(peak, peak_l)
            keep = jnp.exp(peak - newest)
            fresh = jnp.exp(peak_l - newest)
            cur = (num * keep + nums[l][p] * fresh, tot * keep + tots[l][p] * fresh, newest)
        att[:, pl.ds(pl.multiple_of(p * LANES, LANES), LANES)] = (cur[0] / cur[1]).astype(BF16)
        return 0

    lax.fori_loop(0, pairs, join, 0)

    w_load.wait()
    chunk = min(BLOCK, tok)
    chunks = tok // chunk
    other_cols = pl.ds(pl.multiple_of((1 - head) * half, half), half)
    own_cols = pl.ds(pl.multiple_of(head * half, half), half)

    def part_copy(c):
        at = pl.ds(c * chunk, chunk)
        return pltpu.make_async_remote_copy(
            src_ref=psend.at[at], dst_ref=precv.at[at],
            send_sem=psend_sem.at[c], recv_sem=precv_sem.at[c],
            device_id={"head": 1 - head}, device_id_type=MESH)

    for c in range(chunks):
        at = pl.ds(c * chunk, chunk)
        psend[at, :] = jnp.dot(
            att[at, :], w_s[:, other_cols], preferred_element_type=F32).astype(BF16)
        part_copy(c).start()
    for c in range(chunks):
        at = pl.ds(c * chunk, chunk)
        own = jnp.dot(att[at, :], w_s[:, own_cols], preferred_element_type=F32).astype(BF16)
        part_copy(c).wait_recv()
        o_ref[at, :] = (own.astype(F32) + precv[at, :].astype(F32)).astype(BF16)
    for c in range(chunks):
        part_copy(c).wait_send()
    pair_copy.wait_send()
    for l in range(LEVELS):
        for side in (0, 1):
            each(l, side, lambda copy: copy.wait_send())


def local(n_seq, queries, key_rows, value_rows, out_weight):
    tok, columns = queries.shape
    pairs = columns // LANES
    width = out_weight.shape[1]
    half = width // 2
    rows_of = [tok >> l for l in range(LEVELS)]
    assert rows_of[0] % BLOCK == 0 and BLOCK in rows_of
    chunks = tok // min(BLOCK, tok)
    results = [pltpu.VMEM((pairs, r, LANES), F32) for r in rows_of]
    scratch = (
        [pltpu.VMEM((2, pairs, max(r, BLOCK) + 2 * BLOCK, LANES), BF16) for r in rows_of]
        + [pltpu.VMEM((pairs, r, LANES), BF16) for r in rows_of]
        + results * 3
        + [
            pltpu.VMEM((3, tok, LANES), F32),
            pltpu.VMEM((tok, columns), BF16),
            pltpu.VMEM(out_weight.shape, BF16),
            pltpu.VMEM((tok, half), BF16),
            pltpu.VMEM((tok, half), BF16),
            pltpu.SemaphoreType.DMA((4, pairs)),
            pltpu.SemaphoreType.DMA((LEVELS, 2)),
            pltpu.SemaphoreType.DMA((LEVELS, 2)),
            pltpu.SemaphoreType.DMA((2,)),
            pltpu.SemaphoreType.DMA((chunks,)),
            pltpu.SemaphoreType.DMA((chunks,)),
        ]
    )
    return pl.pallas_call(
        functools.partial(kernel, n_seq, tok, pairs),
        out_shape=jax.ShapeDtypeStruct((tok, half), BF16),
        in_specs=[pl.BlockSpec(memory_space=pl.ANY)] * 4,
        out_specs=pl.BlockSpec(memory_space=pltpu.VMEM),
        scratch_shapes=scratch,
        compiler_params=pltpu.CompilerParams(
            collective_id=0, has_side_effects=True, vmem_limit_bytes=56 * 1024 * 1024),
    )(queries, key_rows, value_rows, out_weight)


def solution(mesh):
    return jax.shard_map(
        functools.partial(local, mesh.shape["seq"]),
        mesh=mesh,
        in_specs=(P("seq", "head"), P("seq", "head"), P("seq", "head"), P("head", None)),
        out_specs=P("seq", "head"),
        check_vma=False,
    )
```

```python
import functools
import math

import jax
import jax.numpy as jnp
from jax import lax
from jax.experimental import pallas as pl
from jax.experimental.pallas import tpu as pltpu
from jax.sharding import PartitionSpec as P

HEAD_DIM = 64
BLOCK = 256
LEVELS = 6
LOG_TWO = 0.6931471805599453
NEG_LARGE = -1e30
LANES = 128
MESH = pl.DeviceIdType.MESH
BF16 = jnp.bfloat16
F32 = jnp.float32


def pool_matrix():
    r = lax.broadcasted_iota(jnp.int32, (BLOCK // 2, BLOCK), 0)
    c = lax.broadcasted_iota(jnp.int32, (BLOCK // 2, BLOCK), 1)
    return jnp.where((c == 2 * r) | (c == 2 * r + 1), 0.5, 0.0).astype(BF16)


def pooled(mat_ref, parts):
    rows = parts[0].shape[0]
    mat = mat_ref[pl.ds(0, rows // 2), pl.ds(0, rows)]
    out = jnp.dot(mat, jnp.concatenate(parts, axis=1), preferred_element_type=F32).astype(BF16)
    return [out[:, i * LANES:(i + 1) * LANES] for i in range(len(parts))]


def kernel(n_seq, tok, pairs, q_hbm, k_hbm, v_hbm, w_hbm, o_ref, *scratch):
    scratch = list(scratch)

    def take(count):
        out = scratch[:count]
        del scratch[:count]
        return out

    kv = take(LEVELS)
    qs = take(LEVELS)
    nums = take(LEVELS)
    tots = take(LEVELS)
    mxs = take(LEVELS)
    mat, tmp, att, w_s, psend, precv, load_sem, send_sem, recv_sem, psend_sem, precv_sem = scratch

    me = lax.axis_index("seq")
    head = lax.axis_index("head")
    rows_of = [tok >> l for l in range(LEVELS)]
    span_of = [max(1, BLOCK // r) for r in rows_of]
    half = o_ref.shape[1]

    loads = []
    for p in range(pairs):
        cols = pl.ds(p * LANES, LANES)
        loads.append(pltpu.make_async_copy(
            k_hbm.at[:, cols], kv[0].at[0, p, pl.ds(BLOCK, tok)], load_sem.at[0, p]))
        loads.append(pltpu.make_async_copy(
            v_hbm.at[:, cols], kv[0].at[1, p, pl.ds(BLOCK, tok)], load_sem.at[1, p]))
        loads.append(pltpu.make_async_copy(q_hbm.at[:, cols], qs[0].at[p], load_sem.at[2, p]))
    w_load = pltpu.make_async_copy(w_hbm, w_s, load_sem.at[3, 0])
    for c in loads:
        c.start()
    w_load.start()
    mat[...] = pool_matrix()

    top = span_of[-1]
    top_block = me // top
    top_blocks = n_seq // top
    barrier = pltpu.get_barrier_semaphore()
    pl.semaphore_signal(barrier, inc=1, device_id={"head": 1 - head}, device_id_type=MESH)
    for delta in (-1, 0, 1):
        there = top_block + delta

        @pl.when((there >= 0) & (there < top_blocks))
        def _():
            for j in range(top):
                other = there * top + j

                @pl.when(other != me)
                def _():
                    pl.semaphore_signal(
                        barrier, inc=1, device_id={"seq": other}, device_id_type=MESH)

    exists = []
    for l in range(LEVELS):
        block = me // span_of[l]
        has_left = block >= 1
        has_right = block + 1 < n_seq // span_of[l]
        exists.append((has_left, has_right))
        r = rows_of[l]

        @pl.when(jnp.logical_not(has_left))
        def _():
            kv[l][:, :, pl.ds(0, BLOCK), :] = jnp.zeros((2, pairs, BLOCK, LANES), BF16)

        @pl.when(jnp.logical_not(has_right))
        def _():
            kv[l][:, :, pl.ds(BLOCK + r, BLOCK), :] = jnp.zeros((2, pairs, BLOCK, LANES), BF16)

    around = jnp.minimum(top_block, 1) + jnp.minimum(top_blocks - 1 - top_block, 1)
    pl.semaphore_wait(barrier, top + top * around)

    def copies(l, side):
        r, n = rows_of[l], span_of[l]
        block, place = me // n, lax.rem(me, n)
        if r >= BLOCK:
            length = BLOCK if l == 0 else BLOCK // 2
            if side == 1:
                src, dst = BLOCK + r - BLOCK, 0
            else:
                src = BLOCK + BLOCK - length
                dst = BLOCK + r + BLOCK - length
        else:
            length = r
            src = BLOCK
            dst = place * r + (0 if side == 1 else BLOCK + r)
            dst = pl.multiple_of(dst, r)
        out = []
        for j in range(n):
            target = (block + (1 if side == 1 else -1)) * n + j
            out.append(pltpu.make_async_remote_copy(
                src_ref=kv[l].at[:, :, pl.ds(src, length)],
                dst_ref=kv[l].at[:, :, pl.ds(dst, length)],
                send_sem=send_sem.at[l, side, j],
                recv_sem=recv_sem.at[l, 1 - side],
                device_id={"seq": target},
                device_id_type=MESH))
        return out

    def start(l):
        for side in (0, 1):
            @pl.when(exists[l][side])
            def _():
                for c in copies(l, side):
                    c.start()

    def wait(l):
        r = rows_of[l]
        for side in (0, 1):
            length = BLOCK // 2 if (r >= BLOCK and l > 0) else BLOCK
            if side == 0:
                at = 0
            else:
                at = BLOCK + r + BLOCK - length

            @pl.when(exists[l][side])
            def _():
                region = kv[l].at[:, :, pl.ds(at, length)]
                pltpu.make_async_copy(region, region, recv_sem.at[l, side]).wait()

    for c in loads:
        c.wait()
    start(0)

    for l in range(1, LEVELS):
        r = rows_of[l]
        step = min(BLOCK, 2 * r)

        for p in range(pairs):
            for at in range(0, 2 * r, step):
                to = pl.ds(BLOCK + at // 2, step // 2)
                k, v, q = pooled(mat, [
                    kv[l - 1][0, p, pl.ds(BLOCK + at, step), :],
                    kv[l - 1][1, p, pl.ds(BLOCK + at, step), :],
                    qs[l - 1][p, pl.ds(at, step), :]])
                kv[l][0, p, to, :] = k
                kv[l][1, p, to, :] = v
                qs[l][p, pl.ds(at // 2, step // 2), :] = q
        start(l)

    lane = lax.broadcasted_iota(jnp.int32, (1, LANES), 1)
    low = lane < HEAD_DIM
    masks = [jnp.where(low, 1.0, 0.0).astype(BF16), jnp.where(low, 0.0, 1.0).astype(BF16)]
    scale = HEAD_DIM ** -0.5

    def bias_of(valid):
        return jnp.where(valid, 0.0, NEG_LARGE).astype(F32)

    def scores(l, j, p):
        r = rows_of[l]
        size = min(BLOCK, r)
        has_left, has_right = exists[l]
        blocks = max(1, r // BLOCK)
        if r >= BLOCK:
            left_at, right_at = j * BLOCK, (j + 2) * BLOCK
        else:
            left_at, right_at = 0, BLOCK + r
        left_bias = bias_of(has_left) if j == 0 else None
        right_bias = bias_of(has_right) if j == blocks - 1 else None
        if l == 0:
            segments = [(left_at, left_bias), (left_at + BLOCK, None), (right_at, right_bias)]
        else:
            segments = [(left_at, left_bias), (right_at, right_bias)]
        q = qs[l][p, pl.ds(j * BLOCK, size), :]
        ks = [kv[l][0, p, pl.ds(at, BLOCK), :] for at, _ in segments]
        vs = [kv[l][1, p, pl.ds(at, BLOCK), :] for at, _ in segments]
        sums, v_es = [], []
        for e in (0, 1):
            mine = masks[e]
            other = masks[1 - e]
            q_e = q * (mine * scale) + other
            k_e = []
            for (at, bias), k in zip(segments, ks):
                k = k * mine
                if bias is not None:
                    k = k + (other.astype(F32) * bias).astype(BF16)
                k_e.append(k)
            k_e = jnp.concatenate(k_e, axis=0)
            v_es.append(jnp.concatenate([v * mine + other for v in vs], axis=0))
            sums.append(lax.dot_general(
                q_e, k_e, (((1,), (1,)), ((), ())), preferred_element_type=F32))
        return sums, v_es

    def finish(l, j, p, sums, v_es):
        accs, peaks = [], []
        for s, v_e in zip(sums, v_es):
            peak = jnp.max(s, axis=1, keepdims=True)
            weights = jnp.exp(s - peak).astype(BF16)
            accs.append(jnp.dot(weights, v_e, preferred_element_type=F32))
            peaks.append(peak)
        at = pl.ds(j * BLOCK, min(BLOCK, rows_of[l]))
        nums[l][p, at, :] = jnp.where(low, accs[0], accs[1])
        tots[l][p, at, :] = pltpu.roll(jnp.where(low, accs[1], accs[0]), HEAD_DIM, 1)
        mxs[l][p, at, :] = jnp.where(low, peaks[0], peaks[1]) + l * LOG_TWO

    def phase(which):
        def body(p, _):
            ahead = scores(*which[0], p)
            for i, (l, j) in enumerate(which):
                now = ahead
                if i + 1 < len(which):
                    ahead = scores(*which[i + 1], p)
                finish(l, j, p, *now)
            return 0

        lax.fori_loop(0, pairs, body, 0)

    def near(l):
        r, below = rows_of[l], rows_of[l - 1]

        for p in range(pairs):
            k, v = pooled(mat, [kv[l - 1][s, p, pl.ds(0, BLOCK), :] for s in range(2)])
            kv[l][0, p, pl.ds(BLOCK // 2, BLOCK // 2), :] = k
            kv[l][1, p, pl.ds(BLOCK // 2, BLOCK // 2), :] = v
            k, v = pooled(
                mat, [kv[l - 1][s, p, pl.ds(BLOCK + below, BLOCK), :] for s in range(2)])
            kv[l][0, p, pl.ds(BLOCK + r, BLOCK // 2), :] = k
            kv[l][1, p, pl.ds(BLOCK + r, BLOCK // 2), :] = v

    blocks0 = max(1, tok // BLOCK)
    inner = list(range(1, blocks0 - 1))
    outer = [j for j in range(blocks0) if j not in inner]
    if inner:
        phase([(0, j) for j in inner])
    wait(0)
    phase([(0, j) for j in outer])
    small = []
    for l in range(1, LEVELS):
        wait(l)
        if rows_of[l] >= BLOCK:
            near(l)
        if rows_of[l] > BLOCK:
            phase([(l, j) for j in range(rows_of[l] // BLOCK)])
        else:
            small.append((l, 0))
    phase(small)

    def join(p, _):
        cur = (nums[-1][p], tots[-1][p], mxs[-1][p])
        for l in range(LEVELS - 2, -1, -1):
            r = rows_of[l]
            for i, x in enumerate(cur):
                tmp[i, pl.ds(0, r // 2, stride=2), :] = x
                tmp[i, pl.ds(1, r // 2, stride=2), :] = x
            num, tot, peak = (tmp[i, pl.ds(0, r), :] for i in range(3))
            peak_l = mxs[l][p]
            newest = jnp.maximum(peak, peak_l)
            keep = jnp.exp(peak - newest)
            fresh = jnp.exp(peak_l - newest)
            cur = (num * keep + nums[l][p] * fresh, tot * keep + tots[l][p] * fresh, newest)
        att[:, pl.ds(pl.multiple_of(p * LANES, LANES), LANES)] = (cur[0] / cur[1]).astype(BF16)
        return 0

    lax.fori_loop(0, pairs, join, 0)

    w_load.wait()
    chunk = min(BLOCK, tok)
    chunks = tok // chunk
    other_cols = pl.ds(pl.multiple_of((1 - head) * half, half), half)
    own_cols = pl.ds(pl.multiple_of(head * half, half), half)

    def part_copy(c):
        at = pl.ds(c * chunk, chunk)
        return pltpu.make_async_remote_copy(
            src_ref=psend.at[at], dst_ref=precv.at[at],
            send_sem=psend_sem.at[c], recv_sem=precv_sem.at[c],
            device_id={"head": 1 - head}, device_id_type=MESH)

    for c in range(chunks):
        at = pl.ds(c * chunk, chunk)
        psend[at, :] = jnp.dot(
            att[at, :], w_s[:, other_cols], preferred_element_type=F32).astype(BF16)
        part_copy(c).start()
    for c in range(chunks):
        at = pl.ds(c * chunk, chunk)
        own = jnp.dot(att[at, :], w_s[:, own_cols], preferred_element_type=F32).astype(BF16)
        part_copy(c).wait_recv()
        o_ref[at, :] = (own.astype(F32) + precv[at, :].astype(F32)).astype(BF16)
    for c in range(chunks):
        part_copy(c).wait_send()
    for l in range(LEVELS):
        for side in (0, 1):
            @pl.when(exists[l][side])
            def _():
                for c in copies(l, side):
                    c.wait_send()


def local(n_seq, queries, key_rows, value_rows, out_weight):
    tok, columns = queries.shape
    pairs = columns // LANES
    width = out_weight.shape[1]
    half = width // 2
    rows_of = [tok >> l for l in range(LEVELS)]
    top = max(1, BLOCK // rows_of[-1])
    chunks = tok // min(BLOCK, tok)
    results = [pltpu.VMEM((pairs, r, LANES), F32) for r in rows_of]
    scratch = (
        [pltpu.VMEM((2, pairs, r + 2 * BLOCK, LANES), BF16) for r in rows_of]
        + [pltpu.VMEM((pairs, r, LANES), BF16) for r in rows_of]
        + results * 3
        + [
            pltpu.VMEM((BLOCK // 2, BLOCK), BF16),
            pltpu.VMEM((3, tok, LANES), F32),
            pltpu.VMEM((tok, columns), BF16),
            pltpu.VMEM(out_weight.shape, BF16),
            pltpu.VMEM((tok, half), BF16),
            pltpu.VMEM((tok, half), BF16),
            pltpu.SemaphoreType.DMA((4, pairs)),
            pltpu.SemaphoreType.DMA((LEVELS, 2, top)),
            pltpu.SemaphoreType.DMA((LEVELS, 2)),
            pltpu.SemaphoreType.DMA((chunks,)),
            pltpu.SemaphoreType.DMA((chunks,)),
        ]
    )
    return pl.pallas_call(
        functools.partial(kernel, n_seq, tok, pairs),
        out_shape=jax.ShapeDtypeStruct((tok, half), BF16),
        in_specs=[pl.BlockSpec(memory_space=pl.ANY)] * 4,
        out_specs=pl.BlockSpec(memory_space=pltpu.VMEM),
        scratch_shapes=scratch,
        compiler_params=pltpu.CompilerParams(
            collective_id=0, has_side_effects=True, vmem_limit_bytes=56 * 1024 * 1024),
    )(queries, key_rows, value_rows, out_weight)


def solution(mesh):
    return jax.shard_map(
        functools.partial(local, mesh.shape["seq"]),
        mesh=mesh,
        in_specs=(P("seq", "head"), P("seq", "head"), P("seq", "head"), P("head", None)),
        out_specs=P("seq", "head"),
        check_vma=False,
    )
```
